512 devices in a mesh: dp: 64 (over z_hi, y, core), group: 8 (over x, z_lo).
Axes of the slice: x: 4, y: 8, z: 8 (z_hi: 4, z_lo: 2; z = z_hi * 2 + z_lo), core: 2. Of those that a mesh axis runs over, the one named last changes fastest.
Arguments:
- tokens: bfloat16 [49152, 1024], P('dp'), may hold values from -100 to 100
- cotangent: bfloat16 [49152, 8192], P('dp', 'group'), may hold values from -3 to 3
Outputs:
- update: bfloat16 [1024, 8192], P('dp', 'group')
The draws below stay inside these ranges and needn't reach their ends.
All inputs are finite; a program needn't handle non-finite values.
Results may differ from the reference program's by a relative error of at most 0.0025.
The reference program's roundings to bfloat16 on the way count: a program that leaves them out, or rounds other values in their place, can miss the bound.
Values may be sent and summed in bfloat16 or wider, within the bound.
No kernel may reach another device: no remote copies, remote signals or barrier semaphores. Data moves between devices by JAX's collectives and lax.ppermute only.
A program may use at most 64 MiB of HBM per device.

```python
import math
from functools import partial
import jax
import jax.numpy as jnp
from jax import lax

BLOCK = 1024
ITERS = 2
TILES = 8
TOKENS = 49152


def column_scales(key, length, period, groups):
    position = jnp.arange(length, dtype=jnp.int32)
    inner = (position % period).astype(jnp.float32) / period
    outer = (position // period).astype(jnp.float32) / groups
    jitter = jax.random.uniform(key, (length,), jnp.float32, 0.0, math.log(4.0))
    return jnp.exp(math.log(3.0) * (inner + outer) + jitter)


def draw_tokens(key, part):
    key = jax.random.fold_in(key, 11)
    first, second = jax.random.split(key, 2)
    scales = column_scales(first, BLOCK, BLOCK, 1)
    values = jax.random.truncated_normal(second, -3.0, 3.0, (TOKENS, BLOCK), jnp.float32)
    return (values * scales).astype(jnp.bfloat16)


def draw_cotangent(key, part):
    key = jax.random.fold_in(key, 23)
    first, second = jax.random.split(key, 2)
    scales = 0.01 * column_scales(first, TILES * BLOCK, BLOCK, TILES)
    values = jax.random.truncated_normal(second, -3.0, 3.0, (TOKENS, TILES * BLOCK), jnp.float32)
    return (values * scales).astype(jnp.bfloat16)


def setup_inputs(seed: int = 0) -> dict:
    streams_of = jax.random.split(jax.random.key(seed), 3)
    return {
        "tokens": draw_tokens(jax.random.fold_in(streams_of[2], 71), 0),
        "cotangent": draw_cotangent(jax.random.fold_in(streams_of[2], 71), 0),
    }


def newton_factors(stat):
    identity = jnp.eye(BLOCK, dtype=jnp.float32)
    iterate = (stat / jnp.sqrt(jnp.sum(stat * stat))).astype(jnp.bfloat16)
    factors = []
    for step in range(ITERS):
        factor = ((5.0 * identity - iterate.astype(jnp.float32)) / 4.0).astype(jnp.bfloat16)
        factors.append(factor)
        if step < ITERS - 1:
            for power in range(4):
                iterate = jnp.dot(iterate, factor, preferred_element_type=jnp.float32).astype(jnp.bfloat16)
    return factors

def tile_precond(tokens, cot_tile):
    gradient = lax.dot_general(tokens, cot_tile, (((0,), (0,)), ((), ())), preferred_element_type=jnp.float32)
    gradient_b = gradient.astype(jnp.bfloat16)
    left_stat = lax.dot_general(gradient_b, gradient_b, (((1,), (1,)), ((), ())), preferred_element_type=jnp.float32)
    right_stat = lax.dot_general(gradient_b, gradient_b, (((0,), (0,)), ((), ())), preferred_element_type=jnp.float32)
    left_factors = newton_factors(left_stat)
    right_factors = newton_factors(right_stat)
    left_root = left_factors[0]
    for step in range(1, ITERS):
        left_root = jnp.dot(left_root, left_factors[step], preferred_element_type=jnp.float32).astype(jnp.bfloat16)
    chain = jnp.dot(left_root, gradient_b, preferred_element_type=jnp.float32).astype(jnp.bfloat16)
    for step in range(ITERS - 1):
        chain = jnp.dot(chain, right_factors[step], preferred_element_type=jnp.float32).astype(jnp.bfloat16)
    return jnp.dot(chain, right_factors[ITERS - 1], preferred_element_type=jnp.float32)

def reference(tokens, cotangent):
    tiled = jnp.transpose(cotangent.reshape(TOKENS, TILES, BLOCK), (1, 0, 2))
    precond = lax.map(partial(tile_precond, tokens), tiled)
    mean_square = jnp.sum(precond * precond) / (TILES * BLOCK * BLOCK)
    update = precond / jnp.sqrt(mean_square + 1e-06)
    return jnp.transpose(update, (1, 0, 2)).reshape(BLOCK, TILES * BLOCK).astype(jnp.bfloat16)
```

```python
import jax
import jax.numpy as jnp
from jax import lax
from jax.sharding import PartitionSpec as P

ITERS = 2
Z, Y, C = 4, 8, 2


def dp_perm(dz, dy, dc):
    pairs = []
    for z in range(Z):
        for y in range(Y):
            for c in range(C):
                target = ((z + dz) % Z) * Y * C + ((y + dy) % Y) * C + (c + dc) % C
                pairs.append((z * Y * C + y * C + c, target))
    return pairs


def newton(stat, identity):
    iterate = lax.reduce_precision(stat / jnp.sqrt(jnp.sum(stat * stat)), 8, 7)
    factors = []
    for step in range(ITERS):
        factor = ((5.0 * identity - iterate) / 4.0).astype(jnp.bfloat16)
        factors.append(factor)
        if step < ITERS - 1:
            for power in range(4):
                iterate = lax.reduce_precision(
                    jnp.dot(
                        iterate.astype(jnp.bfloat16), factor, preferred_element_type=jnp.float32
                    ),
                    8,
                    7,
                )
    return factors


def on_device(tokens, cotangent):
    width = tokens.shape[1]
    dp = lax.axis_index("dp")
    z, y, c = dp // (Y * C), (dp // C) % Y, dp % C
    identity = jnp.eye(width, dtype=jnp.float32)
    half = width // C
    slab = half // Y
    part = slab // Z

    partial = lax.dot_general(
        tokens, cotangent, (((0,), (0,)), ((), ())), preferred_element_type=jnp.float32
    )
    away = lax.dynamic_slice_in_dim(partial, (1 - c) * half, half, 0)
    near = lax.dynamic_slice_in_dim(partial, c * half, half, 0)
    near = near + lax.ppermute(away, "dp", dp_perm(0, 0, 1))
    got = []
    for k in range(1, Y):
        piece = lax.dynamic_slice_in_dim(near, ((y + k) % Y) * slab, slab, 0)
        got.append(lax.ppermute(piece, "dp", dp_perm(0, k, 0)))
    own = lax.dynamic_slice_in_dim(near, y * slab, slab, 0)
    for piece in got:
        own = own + piece
    got = []
    for k in range(1, Z):
        piece = lax.dynamic_slice_in_dim(own, ((z + k) % Z) * part, part, 0)
        got.append(lax.ppermute(piece, "dp", dp_perm(k, 0, 0)))
    rows = lax.dynamic_slice_in_dim(own, z * part, part, 0)
    for piece in got:
        rows = rows + piece
    rows = rows.astype(jnp.bfloat16)

    def gather(block, size, me, perm_of):
        pieces = [block] + [lax.ppermute(block, "dp", perm_of(size - k)) for k in range(1, size)]
        order = jnp.stack(pieces)
        twice = jnp.concatenate([order, order])
        whole = lax.dynamic_slice_in_dim(twice, (size - me) % size, size, 0)
        return whole.reshape(size * block.shape[0], block.shape[1])

    rows = gather(rows, Z, z, lambda k: dp_perm(k, 0, 0))
    rows = gather(rows, Y, y, lambda k: dp_perm(0, k, 0))
    gradient = gather(rows, C, c, lambda k: dp_perm(0, 0, k))

    left_stat = lax.dot_general(
        gradient, gradient, (((1,), (1,)), ((), ())), preferred_element_type=jnp.float32
    )
    right_stat = lax.dot_general(
        gradient, gradient, (((0,), (0,)), ((), ())), preferred_element_type=jnp.float32
    )
    left = newton(left_stat, identity)
    right = newton(right_stat, identity)
    chain = left[0]
    for factor in left[1:]:
        chain = jnp.dot(chain, factor, preferred_element_type=jnp.float32).astype(jnp.bfloat16)
    chain = jnp.dot(chain, gradient, preferred_element_type=jnp.float32).astype(jnp.bfloat16)
    for factor in right[:-1]:
        chain = jnp.dot(chain, factor, preferred_element_type=jnp.float32).astype(jnp.bfloat16)
    precond = jnp.dot(chain, right[-1], preferred_element_type=jnp.float32)
    square = jnp.broadcast_to(jnp.sum(precond * precond), (8, 128))
    groups = lax.axis_size("group")
    total = square
    for k in range(1, groups):
        total = total + lax.ppermute(square, "group", [(g, (g + k) % groups) for g in range(groups)])
    mean_square = total[0, 0] / (groups * width * width)
    mine = lax.dynamic_slice_in_dim(precond, dp * part, part, 0)
    return (mine / jnp.sqrt(mean_square + 1e-06)).astype(jnp.bfloat16)


def solution(mesh):
    return jax.shard_map(
        on_device,
        mesh=mesh,
        in_specs=(P("dp", None), P("dp", "group")),
        out_specs=P("dp", "group"),
        check_vma=False,
    )
```

```python
import jax
import jax.numpy as jnp
import numpy as np
from jax import lax
from jax.experimental import pallas as pl
from jax.experimental.pallas import tpu as pltpu
from jax.sharding import Mesh, PartitionSpec as P

Z, Y, C = 4, 8, 2
DP = ("z", "y", "c")
TILE = 256
VMEM = pl.BlockSpec(memory_space=pltpu.VMEM)
SMEM = pl.BlockSpec(memory_space=pltpu.SMEM)
f32, bf16 = jnp.float32, jnp.bfloat16


def device(z, y, c):
    return z * Y * C + y * C + c


FIRST = [[device(z, y, 0) for y in range(Y)] for z in range(Z)] + [
    [device(z, 2 * p + q, 1) for z in range(Z) for q in range(2)] for p in range(Y // 2)
]
SECOND = [[device(z, y, 0) for z in range(Z)] for y in range(Y)] + [
    [device(z, 2 * p + q, 1) for p in range(Y // 2)] for z in range(Z) for q in range(2)
]


def half_product(half, tokens, cotangent):
    depth, width = tokens.shape
    rows = width // C

    def body(half_ref, tokens_ref, cotangent_ref, out_ref, turned):
        turned[...] = tokens_ref[...].T

        @pl.loop(0, width // TILE)
        def _(n):
            columns = pl.ds(pl.multiple_of(n * TILE, TILE), TILE)
            out_ref[:, columns] = jnp.dot(
                turned[...], cotangent_ref[:, columns], preferred_element_type=f32
            )

    return pl.pallas_call(
        body,
        grid_spec=pltpu.PrefetchScalarGridSpec(
            num_scalar_prefetch=1,
            grid=(1,),
            in_specs=[
                pl.BlockSpec((depth, rows), lambda i, half: (0, half[0])),
                pl.BlockSpec((depth, width), lambda i, half: (0, 0)),
            ],
            out_specs=pl.BlockSpec((rows, width), lambda i, half: (0, 0)),
            scratch_shapes=[pltpu.VMEM((rows, depth), bf16)],
        ),
        out_shape=jax.ShapeDtypeStruct((rows, width), f32),
        compiler_params=pltpu.CompilerParams(vmem_limit_bytes=40 * 2**20),
        cost_estimate=pl.CostEstimate(
            flops=2 * depth * rows * width, bytes_accessed=6 * 2**20, transcendentals=0
        ),
        name="half_product",
    )(half, tokens, cotangent)


def precondition(place, mine, theirs):
    half, width = mine.shape
    block = 16
    tiles = width // TILE

    def body(place_ref, mine_ref, theirs_ref, rows_ref, square_ref, g, gt, sl, sr, xl, yl, xr, yr, f0l, f1l, f0r, f1r, h, k):
        core, own = place_ref[0], place_ref[1]
        g[pl.ds(pl.multiple_of(core * half, half), half), :] = mine_ref[...]
        g[pl.ds(pl.multiple_of((1 - core) * half, half), half), :] = theirs_ref[...]

        def at(n):
            return pl.ds(pl.multiple_of(n * TILE, TILE), TILE)

        def fold(square):
            return jnp.sum(square.reshape(-1, 8, square.shape[1]), axis=0)

        def identity(n):
            row = lax.broadcasted_iota(jnp.int32, (width, TILE), 0)
            column = lax.broadcasted_iota(jnp.int32, (width, TILE), 1)
            return row == column + n * TILE

        def factor(iterate, eye):
            return (jnp.where(eye, 5.0 - iterate, -iterate) * 0.25).astype(bf16)

        def stat(a, b, out, n, acc):
            s = jnp.dot(a[...], b[:, at(n)], preferred_element_type=f32)
            out[:, at(n)] = s
            return acc + fold(s * s)

        def first(s, inverse, x, f, n):
            it = (s[:, at(n)] * inverse).astype(bf16)
            x[:, at(n)] = it
            f[:, at(n)] = factor(it.astype(f32), identity(n))

        def power(x, f, out, n):
            out[:, at(n)] = jnp.dot(x[...], f[:, at(n)], preferred_element_type=f32).astype(bf16)

        def last(x, f, out, n):
            it = jnp.dot(x[...], f[:, at(n)], preferred_element_type=f32).astype(bf16)
            out[:, at(n)] = factor(it.astype(f32), identity(n))

        def inverse_norm(acc):
            total = jnp.sum(jnp.sum(acc, axis=0, keepdims=True), axis=1, keepdims=True)
            return 1.0 / jnp.sqrt(total)

        zero = jnp.zeros((8, TILE), f32)

        @pl.loop(0, tiles)
        def _(n):
            gt[:, at(n)] = g[at(n), :].T

        acc = lax.fori_loop(0, tiles, lambda n, a: stat(g, gt, sl, n, a), zero)
        inverse_l = inverse_norm(acc)

        def both(n, a):
            first(sl, inverse_l, xl, f0l, n)
            return stat(gt, g, sr, n, a)

        inverse_r = inverse_norm(lax.fori_loop(0, tiles, both, zero))

        @pl.loop(0, tiles)
        def _(n):
            first(sr, inverse_r, xr, f0r, n)
            power(xl, f0l, yl, n)

        @pl.loop(0, tiles)
        def _(n):
            power(yl, f0l, xl, n)
            power(xr, f0r, yr, n)

        @pl.loop(0, tiles)
        def _(n):
            power(xl, f0l, yl, n)
            power(yr, f0r, xr, n)

        @pl.loop(0, tiles)
        def _(n):
            last(yl, f0l, f1l, n)
            power(xr, f0r, yr, n)

        @pl.loop(0, half // block)
        def _(i):
            source = pl.ds(pl.multiple_of((2 * i + core) * block, block), block)
            h[pl.ds(pl.multiple_of(i * block, block), block), :] = f0l[source, :]

        @pl.loop(0, tiles)
        def _(n):
            last(yr, f0r, f1r, n)
            power(h, f1l, k, n)

        @pl.loop(0, tiles)
        def _(n):
            power(k, g, h, n)

        @pl.loop(0, tiles)
        def _(n):
            power(h, f0r, k, n)

        precond = sl

        def final(n, a):
            p = jnp.dot(k[...], f1r[:, at(n)], preferred_element_type=f32)
            precond[pl.ds(0, half), at(n)] = p
            return a + fold(p * p)

        acc = lax.fori_loop(0, tiles, final, zero)
        square_ref[...] = acc[:, :128] + acc[:, 128:]
        rows_ref[...] = precond[pl.ds(pl.multiple_of(own * block, block), block), :]

    wide, stat_t = pltpu.VMEM((width, width), bf16), pltpu.VMEM((width, width), f32)
    narrow = pltpu.VMEM((half, width), bf16)
    return pl.pallas_call(
        body,
        in_specs=[SMEM, VMEM, VMEM],
        out_specs=[VMEM, VMEM],
        out_shape=[
            jax.ShapeDtypeStruct((block, width), f32),
            jax.ShapeDtypeStruct((8, 128), f32),
        ],
        scratch_shapes=[wide, wide, stat_t, stat_t] + [wide] * 8 + [narrow] * 2,
        compiler_params=pltpu.CompilerParams(vmem_limit_bytes=48 * 2**20),
        cost_estimate=pl.CostEstimate(
            flops=24 * width**3, bytes_accessed=3 * 2**20, transcendentals=0
        ),
        name="precondition",
    )(place, mine, theirs)


def on_device(tokens, cotangent):
    width = tokens.shape[1]
    z, y, c = lax.axis_index("z"), lax.axis_index("y"), lax.axis_index("c")
    half = width // C
    core_swap = [(0, 1), (1, 0)]

    near_half = jnp.full((1,), c, jnp.int32)
    away = half_product(1 - near_half, tokens, cotangent)
    received = lax.ppermute(away, "c", core_swap)
    near = half_product(near_half, tokens, cotangent)
    rows = near + received
    for groups in (FIRST, SECOND):
        count = len(groups[0])
        parts = rows.reshape(count, rows.shape[0] // count, width)
        rows = jnp.sum(lax.all_to_all(parts, DP, 0, 0, axis_index_groups=groups), axis=0)
    rows = rows.astype(bf16)
    for groups in (SECOND, FIRST):
        count = len(groups[0])
        copies = jnp.broadcast_to(rows, (count,) + rows.shape)
        rows = lax.all_to_all(copies, DP, 0, 0, axis_index_groups=groups)
        rows = rows.reshape(count * rows.shape[1], width)
    theirs = lax.ppermute(rows, "c", core_swap)

    place = jnp.stack([c, z * Y + y]).astype(jnp.int32)
    precond, square = precondition(place, rows, theirs)
    square = jnp.broadcast_to(jnp.sum(square), (C * lax.axis_size("group"), 1, 128))
    total = jnp.sum(lax.all_to_all(square, ("c", "group"), 0, 0)[:, 0, 0])
    mean_square = total / (lax.axis_size("group") * width * width)
    return (precond / jnp.sqrt(mean_square + 1e-06)).astype(bf16)


def solution(mesh):
    groups = mesh.shape["group"]
    split = Mesh(np.asarray(mesh.devices).reshape(Z, Y, C, groups), DP + ("group",))
    return jax.shard_map(
        on_device,
        mesh=split,
        in_specs=(P(DP, None), P(DP, "group")),
        out_specs=P(DP, "group"),
        check_vma=False,
    )
```

```python
import jax
import jax.numpy as jnp
import numpy as np
from jax import lax
from jax.experimental import pallas as pl
from jax.experimental.pallas import tpu as pltpu
from jax.sharding import Mesh, PartitionSpec as P

Z, Y, C = 4, 8, 2
DP = ("z", "y", "c")
TILE = 256
VMEM = pl.BlockSpec(memory_space=pltpu.VMEM)
SMEM = pl.BlockSpec(memory_space=pltpu.SMEM)
f32, bf16 = jnp.float32, jnp.bfloat16


def device(z, y, c):
    return z * Y * C + y * C + c


Y_SETS = ((0, 2, 5, 7), (1, 3, 4, 6))
Z_SETS = ((0, 3), (1, 2))


def shifted(v, u, c):
    return device((v + c) % Z, (u + c) % Y, c)


def member(values, pair):
    return [v for v in values if v // 2 == pair][0]


FIRST = [
    [shifted(member(vs, m), member(us, p), c) for vs in Z_SETS for us in Y_SETS]
    for c in range(C)
    for m in range(Z // 2)
    for p in range(Y // 2)
]
SECOND = [
    [shifted(v, u, c) for v in vs for u in us] for c in range(C) for vs in Z_SETS for us in Y_SETS
]


def scalar(value):
    return jnp.full((1,), value, jnp.int32)


def normalise(precond, totals, elements):
    def body(precond_ref, totals_ref, out_ref):
        total = totals_ref[pl.ds(0, 8), :]
        for i in range(1, totals_ref.shape[0] // 8):
            total = total + totals_ref[pl.ds(8 * i, 8), :]
        scale = jnp.sqrt(total[0:1, 0:1] / elements + 1e-06)
        out_ref[...] = (precond_ref[...] / scale).astype(bf16)

    return pl.pallas_call(
        body,
        in_specs=[VMEM, VMEM],
        out_specs=VMEM,
        out_shape=jax.ShapeDtypeStruct(precond.shape, bf16),
        name="normalise",
    )(precond, totals)


def half_product(half, tokens, cotangent):
    depth, width = tokens.shape
    rows = width // C
    tiles, slabs = width // TILE, 3
    slab = depth // slabs

    def body(half_ref, tokens_ref, cotangent_ref, out_ref, held, turned, wide, sems, wide_sems):
        columns = pl.ds(pl.multiple_of(half_ref[0] * rows, rows), rows)
        copies = [
            pltpu.make_async_copy(
                tokens_ref.at[pl.ds(i * slab, slab), columns],
                held.at[pl.ds(i * slab, slab), :],
                sems.at[i],
            )
            for i in range(slabs)
        ] + [
            pltpu.make_async_copy(
                cotangent_ref.at[:, pl.ds(n * TILE, TILE)],
                wide.at[:, pl.ds(n * TILE, TILE)],
                wide_sems.at[n],
            )
            for n in range(tiles)
        ]
        for copy in copies:
            copy.start()
        for i in range(slabs):
            copies[i].wait()
            turned[:, pl.ds(i * slab, slab)] = held[pl.ds(i * slab, slab), :].T
        for n in range(tiles):
            copies[slabs + n].wait()
            here = pl.ds(n * TILE, TILE)
            out_ref[:, here] = jnp.dot(turned[...], wide[:, here], preferred_element_type=f32)

    return pl.pallas_call(
        body,
        in_specs=[SMEM, pl.BlockSpec(memory_space=pl.ANY), pl.BlockSpec(memory_space=pl.ANY)],
        out_specs=VMEM,
        out_shape=jax.ShapeDtypeStruct((rows, width), f32),
        scratch_shapes=[
            pltpu.VMEM((depth, rows), bf16),
            pltpu.VMEM((rows, depth), bf16),
            pltpu.VMEM((depth, width), bf16),
            pltpu.SemaphoreType.DMA((slabs,)),
            pltpu.SemaphoreType.DMA((tiles,)),
        ],
        compiler_params=pltpu.CompilerParams(vmem_limit_bytes=40 * 2**20),
        cost_estimate=pl.CostEstimate(
            flops=2 * depth * rows * width, bytes_accessed=6 * 2**20, transcendentals=0
        ),
        name="half_product",
    )(half, tokens, cotangent)


def precondition(place, mine, theirs, copies):
    half, width = mine.shape
    block = 16
    lo, hi = pl.ds(0, half), pl.ds(half, half)

    def body(place_ref, mine_ref, theirs_ref, rows_ref, square_ref, g, gt, sl, sr, xl, yl, xr, yr, f0l, f1l, f0r, f1r, h, k):
        core, own = place_ref[0], place_ref[1]
        g[pl.ds(pl.multiple_of(core * half, half), half), :] = mine_ref[...]
        g[pl.ds(pl.multiple_of((1 - core) * half, half), half), :] = theirs_ref[...]
        row = lax.broadcasted_iota(jnp.int32, (half, half), 0)
        column = lax.broadcasted_iota(jnp.int32, (half, half), 1)
        eye = row == column

        def dot(a, b):
            return jnp.dot(a, b, preferred_element_type=f32)

        def fold(square):
            return jnp.sum(square.reshape(-1, 8, square.shape[1]), axis=0)

        def factor(iterate, diagonal):
            if not diagonal:
                return (iterate * -0.25).astype(bf16)
            return (jnp.where(eye, 5.0 - iterate, -iterate) * 0.25).astype(bf16)

        def stat(a, b, out):
            s = dot(a[lo, :], b[:, lo])
            out[lo, lo] = s
            acc = fold(s * s)
            s = dot(a[lo, :], b[:, hi])
            out[lo, hi] = s
            acc = acc + 2.0 * fold(s * s)
            s = dot(a[hi, :], b[:, hi])
            out[hi, hi] = s
            acc = acc + fold(s * s)
            total = jnp.sum(jnp.sum(acc, axis=0, keepdims=True), axis=1, keepdims=True)
            return 1.0 / jnp.sqrt(total)

        def first(s, inverse, x, f):
            for r, c in ((lo, lo), (lo, hi), (hi, hi)):
                it = (s[r, c] * inverse).astype(bf16)
                x[r, c] = it
                fac = factor(it.astype(f32), r is c)
                f[r, c] = fac
                if r is not c:
                    x[c, r] = it.T
                    f[c, r] = fac.T

        def power(x, f, out):
            out[lo, lo] = dot(x[lo, :], f[:, lo]).astype(bf16)
            p = dot(x[...], f[:, hi]).astype(bf16)
            out[:, hi] = p
            out[hi, lo] = p[:half].T

        def last(x, f, out):
            it = dot(x[lo, :], f[:, lo]).astype(bf16)
            out[lo, lo] = factor(it.astype(f32), True)
            it = dot(x[...], f[:, hi]).astype(bf16).astype(f32)
            fac = factor(it[:half], False)
            out[lo, hi] = fac
            out[hi, lo] = fac.T
            out[hi, hi] = factor(it[half:], True)

        def times(x, f, out):
            for c in (lo, hi):
                out[:, c] = dot(x[...], f[:, c]).astype(bf16)

        gt[:, lo] = g[lo, :].T
        gt[:, hi] = g[hi, :].T
        inverse_l = stat(g, gt, sl)
        first(sl, inverse_l, xl, f0l)
        inverse_r = stat(gt, g, sr)
        power(xl, f0l, yl)
        first(sr, inverse_r, xr, f0r)
        power(yl, f0l, xl)
        power(xr, f0r, yr)
        power(xl, f0l, yl)
        power(yr, f0r, xr)
        last(yl, f0l, f1l)
        power(xr, f0r, yr)

        for i in range(half // block):
            source = pl.ds(pl.multiple_of((2 * i + core) * block, block), block)
            h[pl.ds(i * block, block), :] = f0l[source, :]
        times(h, f1l, k)
        last(yr, f0r, f1r)
        times(k, g, h)
        times(h, f0r, k)
        precond = sl
        acc = jnp.zeros((8, half), f32)
        for c in (lo, hi):
            p = dot(k[...], f1r[:, c])
            precond[lo, c] = p
            acc = acc + fold(p * p)
        total = jnp.sum(jnp.sum(acc, axis=0, keepdims=True), axis=1, keepdims=True)
        square_ref[...] = jnp.broadcast_to(total, square_ref.shape)
        rows_ref[...] = precond[pl.ds(pl.multiple_of(own * block, block), block), :]

    wide, stat_t = pltpu.VMEM((width, width), bf16), pltpu.VMEM((width, width), f32)
    narrow = pltpu.VMEM((half, width), bf16)
    return pl.pallas_call(
        body,
        in_specs=[SMEM, VMEM, VMEM],
        out_specs=[VMEM, VMEM],
        out_shape=[
            jax.ShapeDtypeStruct((block, width), f32),
            jax.ShapeDtypeStruct((8 * copies, 128), f32),
        ],
        scratch_shapes=[wide, wide, stat_t, stat_t] + [wide] * 8 + [narrow] * 2,
        compiler_params=pltpu.CompilerParams(vmem_limit_bytes=48 * 2**20),
        cost_estimate=pl.CostEstimate(
            flops=20 * width**3, bytes_accessed=3 * 2**20, transcendentals=0
        ),
        name="precondition",
    )(place, mine, theirs)


def on_device(tokens, cotangent):
    width = tokens.shape[1]
    z, y, c = lax.axis_index("z"), lax.axis_index("y"), lax.axis_index("c")
    core_swap = [(0, 1), (1, 0)]

    away = half_product(scalar(1 - c), tokens, cotangent)
    received = lax.ppermute(away, "c", core_swap)
    rows = half_product(scalar(c), tokens, cotangent) + received
    for groups in (FIRST, SECOND):
        count = len(groups[0])
        parts = rows.reshape(count, rows.shape[0] // count, width)
        rows = jnp.sum(lax.all_to_all(parts, DP, 0, 0, axis_index_groups=groups), axis=0)
    rows = rows.astype(bf16)
    for groups in (SECOND, FIRST):
        count = len(groups[0])
        copies = jnp.broadcast_to(rows, (count,) + rows.shape)
        rows = lax.all_to_all(copies, DP, 0, 0, axis_index_groups=groups)
        rows = rows.reshape(count * rows.shape[1], width)
    theirs = lax.ppermute(rows, "c", core_swap)

    groups = lax.axis_size("group")
    place = jnp.stack([c, z * Y + y]).astype(jnp.int32)
    precond, square = precondition(place, rows, theirs, C * groups)
    square = square.reshape(C * groups, 8, 128)
    totals = lax.all_to_all(square, ("c", "group"), 0, 0).reshape(C * groups * 8, 128)
    return normalise(precond, totals, groups * width * width)


def solution(mesh):
    groups = mesh.shape["group"]
    split = Mesh(np.asarray(mesh.devices).reshape(Z, Y, C, groups), DP + ("group",))
    return jax.shard_map(
        on_device,
        mesh=split,
        in_specs=(P(DP, None), P(DP, "group")),
        out_specs=P(DP, "group"),
        check_vma=False,
    )
```

```python
import jax
import jax.numpy as jnp
import numpy as np
from jax import lax
from jax.experimental import pallas as pl
from jax.experimental.pallas import tpu as pltpu
from jax.sharding import Mesh, PartitionSpec as P

Z, Y, C = 4, 8, 2
DP = ("z", "y", "c")
TILE = 256
VMEM = pl.BlockSpec(memory_space=pltpu.VMEM)
SMEM = pl.BlockSpec(memory_space=pltpu.SMEM)
HBM = pl.BlockSpec(memory_space=pltpu.HBM)
f32, bf16 = jnp.float32, jnp.bfloat16


def device(z, y, c):
    return z * Y * C + y * C + c


Y_SETS = ((0, 2, 5, 7), (1, 3, 4, 6))
Z_SETS = ((0, 3), (1, 2))


def shifted(v, u, c):
    return device((v + c) % Z, (u + c) % Y, c)


def member(values, pair):
    return [v for v in values if v // 2 == pair][0]


FIRST = [
    [shifted(member(vs, m), member(us, p), c) for vs in Z_SETS for us in Y_SETS]
    for c in range(C)
    for m in range(Z // 2)
    for p in range(Y // 2)
]
SECOND = [
    [shifted(v, u, c) for v in vs for u in us] for c in range(C) for vs in Z_SETS for us in Y_SETS
]


def scalar(value):
    return jnp.full((1,), value, jnp.int32)


def normalise(precond, totals, elements):
    def body(precond_ref, totals_ref, out_ref):
        total = totals_ref[pl.ds(0, 8), :]
        for i in range(1, totals_ref.shape[0] // 8):
            total = total + totals_ref[pl.ds(8 * i, 8), :]
        scale = jnp.sqrt(total[0:1, 0:1] / elements + 1e-06)
        out_ref[...] = (precond_ref[...] / scale).astype(bf16)

    return pl.pallas_call(
        body,
        in_specs=[VMEM, VMEM],
        out_specs=VMEM,
        out_shape=jax.ShapeDtypeStruct(precond.shape, bf16),
        compiler_params=pltpu.CompilerParams(vmem_limit_bytes=4 * 2**20),
        name="normalise",
    )(precond, totals)


def half_product(half, tokens, cotangent):
    depth, width = tokens.shape
    rows = width // C

    def body(half_ref, tokens_ref, cotangent_ref, out_ref, turned):
        turned[...] = tokens_ref[...].T

        @pl.loop(0, width // TILE)
        def _(n):
            columns = pl.ds(pl.multiple_of(n * TILE, TILE), TILE)
            out_ref[:, columns] = jnp.dot(
                turned[...], cotangent_ref[:, columns], preferred_element_type=f32
            )

    return pl.pallas_call(
        body,
        grid_spec=pltpu.PrefetchScalarGridSpec(
            num_scalar_prefetch=1,
            grid=(1,),
            in_specs=[
                pl.BlockSpec((depth, rows), lambda i, half: (0, half[0])),
                pl.BlockSpec((depth, width), lambda i, half: (0, 0)),
            ],
            out_specs=pl.BlockSpec((rows, width), lambda i, half: (0, 0)),
            scratch_shapes=[pltpu.VMEM((rows, depth), bf16)],
        ),
        out_shape=jax.ShapeDtypeStruct((rows, width), f32),
        compiler_params=pltpu.CompilerParams(vmem_limit_bytes=40 * 2**20),
        cost_estimate=pl.CostEstimate(
            flops=2 * depth * rows * width, bytes_accessed=6 * 2**20, transcendentals=0
        ),
        name="half_product",
    )(half, tokens, cotangent)


def first_product(half, tokens, cotangent):
    depth, width = tokens.shape
    rows = width // C
    tiles, slabs = width // TILE, 3
    slab = depth // slabs

    def body(half_ref, tokens_ref, cotangent_ref, out_ref, held, turned, wide, total, sems, wide_sems, out_sems):
        columns = pl.ds(pl.multiple_of(half_ref[0] * rows, rows), rows)
        copies = [
            pltpu.make_async_copy(
                tokens_ref.at[pl.ds(i * slab, slab), columns],
                held.at[pl.ds(i * slab, slab), :],
                sems.at[i],
            )
            for i in range(slabs)
        ] + [
            pltpu.make_async_copy(
                cotangent_ref.at[:, pl.ds(n * TILE, TILE)],
                wide.at[:, pl.ds(n * TILE, TILE)],
                wide_sems.at[n],
            )
            for n in range(tiles)
        ]
        for copy in copies:
            copy.start()
        for i in range(slabs):
            copies[i].wait()
            turned[:, pl.ds(i * slab, slab)] = held[pl.ds(i * slab, slab), :].T
        out_copies = []
        for n in range(tiles):
            copies[slabs + n].wait()
            here = pl.ds(n * TILE, TILE)
            total[:, here] = jnp.dot(turned[...], wide[:, here], preferred_element_type=f32)
            out_copies.append(
                pltpu.make_async_copy(total.at[:, here], out_ref.at[:, here], out_sems.at[n])
            )
            out_copies[n].start()
        for copy in out_copies:
            copy.wait()

    return pl.pallas_call(
        body,
        in_specs=[SMEM, HBM, HBM],
        out_specs=HBM,
        out_shape=jax.ShapeDtypeStruct((rows, width), f32),
        scratch_shapes=[
            pltpu.VMEM((depth, rows), bf16),
            pltpu.VMEM((rows, depth), bf16),
            pltpu.VMEM((depth, width), bf16),
            pltpu.VMEM((rows, width), f32),
            pltpu.SemaphoreType.DMA((slabs,)),
            pltpu.SemaphoreType.DMA((tiles,)),
            pltpu.SemaphoreType.DMA((tiles,)),
        ],
        compiler_params=pltpu.CompilerParams(vmem_limit_bytes=61_000_000),
        cost_estimate=pl.CostEstimate(
            flops=2 * depth * rows * width, bytes_accessed=6 * 2**20, transcendentals=0
        ),
        name="first_product",
    )(half, tokens, cotangent)


def precondition(place, mine, theirs, copies):
    half, width = mine.shape
    block = 16
    lo, hi = pl.ds(0, half), pl.ds(half, half)

    def body(place_ref, mine_ref, theirs_ref, rows_ref, square_ref, g, gt, sl, sr, xl, yl, xr, yr, f0l, f1l, f0r, f1r, h, k):
        core, own = place_ref[0], place_ref[1]
        g[pl.ds(pl.multiple_of(core * half, half), half), :] = mine_ref[...]
        g[pl.ds(pl.multiple_of((1 - core) * half, half), half), :] = theirs_ref[...]
        row = lax.broadcasted_iota(jnp.int32, (half, half), 0)
        column = lax.broadcasted_iota(jnp.int32, (half, half), 1)
        eye = row == column

        def dot(a, b):
            return jnp.dot(a, b, preferred_element_type=f32)

        def fold(square):
            return jnp.sum(square.reshape(-1, 8, square.shape[1]), axis=0)

        def factor(iterate, diagonal):
            if not diagonal:
                return (iterate * -0.25).astype(bf16)
            return (jnp.where(eye, 5.0 - iterate, -iterate) * 0.25).astype(bf16)

        def stat(a, b, out):
            s = dot(a[lo, :], b[:, lo])
            out[lo, lo] = s
            acc = fold(s * s)
            s = dot(a[lo, :], b[:, hi])
            out[lo, hi] = s
            acc = acc + 2.0 * fold(s * s)
            s = dot(a[hi, :], b[:, hi])
            out[hi, hi] = s
            acc = acc + fold(s * s)
            total = jnp.sum(jnp.sum(acc, axis=0, keepdims=True), axis=1, keepdims=True)
            return 1.0 / jnp.sqrt(total)

        def first(s, inverse, x, f):
            for r, c in ((lo, lo), (lo, hi), (hi, hi)):
                it = (s[r, c] * inverse).astype(bf16)
                x[r, c] = it
                fac = factor(it.astype(f32), r is c)
                f[r, c] = fac
                if r is not c:
                    x[c, r] = it.T
                    f[c, r] = fac.T

        def power(x, f, out):
            for c in (lo, hi):
                out[:, c] = dot(x[...], f[:, c]).astype(bf16)

        def last(x, f, out):
            for c in (lo, hi):
                it = dot(x[...], f[:, c]).astype(bf16).astype(f32)
                out[lo, c] = factor(it[:half], c is lo)
                out[hi, c] = factor(it[half:], c is hi)

        gt[:, lo] = g[lo, :].T
        gt[:, hi] = g[hi, :].T
        inverse_l = stat(g, gt, sl)
        first(sl, inverse_l, xl, f0l)
        inverse_r = stat(gt, g, sr)
        power(xl, f0l, yl)
        first(sr, inverse_r, xr, f0r)
        power(yl, f0l, xl)
        power(xr, f0r, yr)
        power(xl, f0l, yl)
        power(yr, f0r, xr)
        last(yl, f0l, f1l)
        power(xr, f0r, yr)

        for i in range(half // block):
            source = pl.ds(pl.multiple_of((2 * i + core) * block, block), block)
            h[pl.ds(i * block, block), :] = f0l[source, :]
        power(h, f1l, k)
        last(yr, f0r, f1r)
        power(k, g, h)
        power(h, f0r, k)
        precond = sl
        acc = jnp.zeros((8, half), f32)
        for c in (lo, hi):
            p = dot(k[...], f1r[:, c])
            precond[lo, c] = p
            acc = acc + fold(p * p)
        total = jnp.sum(jnp.sum(acc, axis=0, keepdims=True), axis=1, keepdims=True)
        square_ref[...] = jnp.broadcast_to(total, square_ref.shape)
        rows_ref[...] = precond[pl.ds(pl.multiple_of(own * block, block), block), :]

    wide, stat_t = pltpu.VMEM((width, width), bf16), pltpu.VMEM((width, width), f32)
    narrow = pltpu.VMEM((half, width), bf16)
    return pl.pallas_call(
        body,
        in_specs=[SMEM, VMEM, VMEM],
        out_specs=[VMEM, VMEM],
        out_shape=[
            jax.ShapeDtypeStruct((block, width), f32),
            jax.ShapeDtypeStruct((8 * copies, 128), f32),
        ],
        scratch_shapes=[wide, wide, stat_t, stat_t] + [wide] * 8 + [narrow] * 2,
        compiler_params=pltpu.CompilerParams(vmem_limit_bytes=48 * 2**20),
        cost_estimate=pl.CostEstimate(
            flops=23 * width**3, bytes_accessed=3 * 2**20, transcendentals=0
        ),
        name="precondition",
    )(place, mine, theirs)


def on_device(tokens, cotangent):
    width = tokens.shape[1]
    z, y, c = lax.axis_index("z"), lax.axis_index("y"), lax.axis_index("c")
    core_swap = [(0, 1), (1, 0)]

    away = first_product(scalar(1 - c), tokens, cotangent)
    received = lax.ppermute(away, "c", core_swap)
    rows = half_product(scalar(c), tokens, cotangent) + received
    for groups in (FIRST, SECOND):
        count = len(groups[0])
        parts = rows.reshape(count, rows.shape[0] // count, width)
        rows = jnp.sum(lax.all_to_all(parts, DP, 0, 0, axis_index_groups=groups), axis=0)
    rows = rows.astype(bf16)
    for groups in (SECOND, FIRST):
        count = len(groups[0])
        copies = jnp.broadcast_to(rows, (count,) + rows.shape)
        rows = lax.all_to_all(copies, DP, 0, 0, axis_index_groups=groups)
        rows = rows.reshape(count * rows.shape[1], width)
    theirs = lax.ppermute(rows, "c", core_swap)

    groups = lax.axis_size("group")
    place = jnp.stack([c, z * Y + y]).astype(jnp.int32)
    precond, square = precondition(place, rows, theirs, C * groups)
    square = square.reshape(C * groups, 8, 128)
    totals = lax.all_to_all(square, ("c", "group"), 0, 0).reshape(C * groups * 8, 128)
    return normalise(precond, totals, groups * width * width)


def solution(mesh):
    groups = mesh.shape["group"]
    split = Mesh(np.asarray(mesh.devices).reshape(Z, Y, C, groups), DP + ("group",))
    return jax.shard_map(
        on_device,
        mesh=split,
        in_specs=(P(DP, None), P(DP, "group")),
        out_specs=P(DP, "group"),
        check_vma=False,
    )
```

```python
import jax
import jax.numpy as jnp
import numpy as np
from jax import lax
from jax.experimental import pallas as pl
from jax.experimental.pallas import tpu as pltpu
from jax.sharding import Mesh, PartitionSpec as P

Z, Y, C = 4, 8, 2
DP = ("z", "y", "c")
TILE = 512
VMEM = pl.BlockSpec(memory_space=pltpu.VMEM)
SMEM = pl.BlockSpec(memory_space=pltpu.SMEM)
f32, bf16 = jnp.float32, jnp.bfloat16


def device(z, y, c):
    return z * Y * C + y * C + c


Y_SETS = ((0, 2, 5, 7), (1, 3, 4, 6))
Z_SETS = ((0, 3), (1, 2))


def shifted(v, u, c):
    return device((v + c) % Z, (u + c) % Y, c)


def member(values, pair):
    return [v for v in values if v // 2 == pair][0]


FIRST = [
    [shifted(member(vs, m), member(us, p), c) for vs in Z_SETS for us in Y_SETS]
    for c in range(C)
    for m in range(Z // 2)
    for p in range(Y // 2)
]
SECOND = [
    [shifted(v, u, c) for v in vs for u in us] for c in range(C) for vs in Z_SETS for us in Y_SETS
]


def scalar(value):
    return jnp.full((1,), value, jnp.int32)


def normalise(precond, totals, elements):
    def body(precond_ref, totals_ref, out_ref):
        total = totals_ref[pl.ds(0, 8), :]
        for i in range(1, totals_ref.shape[0] // 8):
            total = total + totals_ref[pl.ds(8 * i, 8), :]
        scale = jnp.sqrt(total[0:1, 0:1] / elements + 1e-06)
        out_ref[...] = (precond_ref[...] / scale).astype(bf16)

    return pl.pallas_call(
        body,
        in_specs=[VMEM, VMEM],
        out_specs=VMEM,
        out_shape=jax.ShapeDtypeStruct(precond.shape, bf16),
        compiler_params=pltpu.CompilerParams(vmem_limit_bytes=4 * 2**20),
        name="normalise",
    )(precond, totals)


def half_product(half, tokens, cotangent):
    depth, width = tokens.shape
    rows = width // C

    def body(half_ref, tokens_ref, cotangent_ref, out_ref, turned):
        turned[...] = tokens_ref[...].T

        for n in range(width // TILE):
            columns = pl.ds(n * TILE, TILE)
            out_ref[:, columns] = jnp.dot(
                turned[...], cotangent_ref[:, columns], preferred_element_type=f32
            )

    return pl.pallas_call(
        body,
        grid_spec=pltpu.PrefetchScalarGridSpec(
            num_scalar_prefetch=1,
            grid=(1,),
            in_specs=[
                pl.BlockSpec((depth, rows), lambda i, half: (0, half[0])),
                pl.BlockSpec((depth, width), lambda i, half: (0, 0)),
            ],
            out_specs=pl.BlockSpec((rows, width), lambda i, half: (0, 0)),
            scratch_shapes=[pltpu.VMEM((rows, depth), bf16)],
        ),
        out_shape=jax.ShapeDtypeStruct((rows, width), f32),
        compiler_params=pltpu.CompilerParams(vmem_limit_bytes=40 * 2**20),
        cost_estimate=pl.CostEstimate(
            flops=2 * depth * rows * width, bytes_accessed=6 * 2**20, transcendentals=0
        ),
        name="half_product",
    )(half, tokens, cotangent)


def dot(a, b):
    return jnp.dot(a, b, preferred_element_type=f32)


def fold(square):
    return jnp.sum(square.reshape(-1, 8, square.shape[1]), axis=0)


def own_share(mine):
    half, width = mine.shape
    lo, hi = pl.ds(0, half), pl.ds(half, half)

    def body(mine_ref, turned_ref, right_ref, left_ref):
        turned_ref[...] = mine_ref[...].T
        left_ref[...] = dot(mine_ref[...], turned_ref[...])
        right_ref[lo, lo] = dot(turned_ref[lo, :], mine_ref[:, lo])
        right_ref[:, hi] = dot(turned_ref[...], mine_ref[:, hi])

    return pl.pallas_call(
        body,
        in_specs=[VMEM],
        out_specs=[VMEM, VMEM, VMEM],
        out_shape=[
            jax.ShapeDtypeStruct((width, half), bf16),
            jax.ShapeDtypeStruct((width, width), f32),
            jax.ShapeDtypeStruct((half, half), f32),
        ],
        compiler_params=pltpu.CompilerParams(vmem_limit_bytes=24 * 2**20),
        cost_estimate=pl.CostEstimate(
            flops=2 * width**3, bytes_accessed=2**20, transcendentals=0
        ),
        name="own_share",
    )(mine)


def precondition(place, mine, theirs, turned, right, left, copies):
    half, width = mine.shape
    block = 16
    lo, hi = pl.ds(0, half), pl.ds(half, half)

    def body(place_ref, mine_ref, theirs_ref, turned_ref, right_ref, left_ref, rows_ref, square_ref, g, gt, sl, sr, xl, yl, xr, yr, f0l, f1l, f0r, f1r, h, k, theirs_turned):
        core, own = place_ref[0], place_ref[1]
        ours = pl.ds(pl.multiple_of(core * half, half), half)
        others = pl.ds(pl.multiple_of((1 - core) * half, half), half)
        g[ours, :] = mine_ref[...]
        g[others, :] = theirs_ref[...]
        row = lax.broadcasted_iota(jnp.int32, (half, half), 0)
        column = lax.broadcasted_iota(jnp.int32, (half, half), 1)
        eye = row == column

        def factor(iterate, diagonal):
            if not diagonal:
                return (iterate * -0.25).astype(bf16)
            return (jnp.where(eye, 5.0 - iterate, -iterate) * 0.25).astype(bf16)

        def inverse_norm(diagonal, above):
            acc = 2.0 * fold(above * above)
            for s in diagonal:
                acc = acc + fold(s * s)
            total = jnp.sum(jnp.sum(acc, axis=0, keepdims=True), axis=1, keepdims=True)
            return 1.0 / jnp.sqrt(total)

        def left_stat():
            s = dot(theirs_ref[...], theirs_turned[...])
            sl[others, others] = s
            sl[ours, ours] = left_ref[...]
            above = dot(g[lo, :], gt[:, hi])
            sl[lo, hi] = above
            return inverse_norm([s, left_ref[...]], above)

        def right_stat():
            first_block = right_ref[lo, lo] + dot(theirs_turned[lo, :], theirs_ref[:, lo])
            sr[lo, lo] = first_block
            s = right_ref[:, hi] + dot(theirs_turned[...], theirs_ref[:, hi])
            sr[:, hi] = s
            return inverse_norm([first_block, s[half:]], s[:half])

        def first(s, inverse, x, f):
            for r, c in ((lo, lo), (lo, hi), (hi, hi)):
                it = (s[r, c] * inverse).astype(bf16)
                x[r, c] = it
                fac = factor(it.astype(f32), r is c)
                f[r, c] = fac
                if r is not c:
                    x[c, r] = it.T
                    f[c, r] = fac.T

        def power(x, f, out):
            for c in (lo, hi):
                out[:, c] = dot(x[...], f[:, c]).astype(bf16)

        def last(x, f, out):
            for c in (lo, hi):
                it = dot(x[...], f[:, c]).astype(bf16).astype(f32)
                out[lo, c] = factor(it[:half], c is lo)
                out[hi, c] = factor(it[half:], c is hi)

        theirs_turned[...] = theirs_ref[...].T
        gt[:, ours] = turned_ref[...]
        gt[:, others] = theirs_turned[...]
        inverse_l = left_stat()
        first(sl, inverse_l, xl, f0l)
        inverse_r = right_stat()
        power(xl, f0l, yl)
        first(sr, inverse_r, xr, f0r)
        power(yl, f0l, xl)
        power(xr, f0r, yr)
        power(xl, f0l, yl)
        power(yr, f0r, xr)
        last(yl, f0l, f1l)
        power(xr, f0r, yr)

        for i in range(half // block):
            source = pl.ds(pl.multiple_of((2 * i + core) * block, block), block)
            h[pl.ds(i * block, block), :] = f0l[source, :]
        power(h, f1l, k)
        last(yr, f0r, f1r)
        power(k, g, h)
        power(h, f0r, k)
        precond = sl
        acc = jnp.zeros((8, half), f32)
        for c in (lo, hi):
            p = dot(k[...], f1r[:, c])
            precond[lo, c] = p
            acc = acc + fold(p * p)
        total = jnp.sum(jnp.sum(acc, axis=0, keepdims=True), axis=1, keepdims=True)
        square_ref[...] = jnp.broadcast_to(total, square_ref.shape)
        rows_ref[...] = precond[pl.ds(pl.multiple_of(own * block, block), block), :]

    wide, stat_t = pltpu.VMEM((width, width), bf16), pltpu.VMEM((width, width), f32)
    narrow = pltpu.VMEM((half, width), bf16)
    return pl.pallas_call(
        body,
        in_specs=[SMEM] + [VMEM] * 5,
        out_specs=[VMEM, VMEM],
        out_shape=[
            jax.ShapeDtypeStruct((block, width), f32),
            jax.ShapeDtypeStruct((8 * copies, 128), f32),
        ],
        scratch_shapes=[wide, wide, stat_t, stat_t] + [wide] * 8 + [narrow] * 2 + [pltpu.VMEM((width, half), bf16)],
        compiler_params=pltpu.CompilerParams(vmem_limit_bytes=44 * 2**20),
        cost_estimate=pl.CostEstimate(
            flops=23 * width**3, bytes_accessed=3 * 2**20, transcendentals=0
        ),
        name="precondition",
    )(place, mine, theirs, turned, right, left)


def on_device(tokens, cotangent):
    width = tokens.shape[1]
    z, y, c = lax.axis_index("z"), lax.axis_index("y"), lax.axis_index("c")
    core_swap = [(0, 1), (1, 0)]

    away = half_product(scalar(1 - c), tokens, cotangent)
    received = lax.ppermute(away, "c", core_swap)
    rows = half_product(scalar(c), tokens, cotangent) + received
    for groups in (FIRST, SECOND):
        count = len(groups[0])
        parts = rows.reshape(count, rows.shape[0] // count, width)
        rows = jnp.sum(lax.all_to_all(parts, DP, 0, 0, axis_index_groups=groups), axis=0)
    rows = rows.astype(bf16)
    for groups in (SECOND, FIRST):
        count = len(groups[0])
        copies = jnp.broadcast_to(rows, (count,) + rows.shape)
        rows = lax.all_to_all(copies, DP, 0, 0, axis_index_groups=groups)
        rows = rows.reshape(count * rows.shape[1], width)
    theirs = lax.ppermute(rows, "c", core_swap)

    groups = lax.axis_size("group")
    place = jnp.stack([c, z * Y + y]).astype(jnp.int32)
    precond, square = precondition(place, rows, theirs, *own_share(rows), C * groups)
    square = square.reshape(C * groups, 8, 128)
    totals = lax.all_to_all(square, ("c", "group"), 0, 0).reshape(C * groups * 8, 128)
    return normalise(precond, totals, groups * width * width)


def solution(mesh):
    groups = mesh.shape["group"]
    split = Mesh(np.asarray(mesh.devices).reshape(Z, Y, C, groups), DP + ("group",))
    return jax.shard_map(
        on_device,
        mesh=split,
        in_specs=(P(DP, None), P(DP, "group")),
        out_specs=P(DP, "group"),
        check_vma=False,
    )
```

```python
import jax
import jax.numpy as jnp
import numpy as np
from jax import lax
from jax.experimental import pallas as pl
from jax.experimental.pallas import tpu as pltpu
from jax.sharding import Mesh, PartitionSpec as P

Z, Y, C = 4, 8, 2
DP = ("z", "y", "c")
TILE = 512
VMEM = pl.BlockSpec(memory_space=pltpu.VMEM)
SMEM = pl.BlockSpec(memory_space=pltpu.SMEM)
f32, bf16 = jnp.float32, jnp.bfloat16


def device(z, y, c):
    return z * Y * C + y * C + c


Y_SETS = ((0, 2, 5, 7), (1, 3, 4, 6))
Z_SETS = ((0, 3), (1, 2))


def shifted(v, u, c):
    return device((v + c) % Z, (u + c) % Y, c)


def member(values, pair):
    return [v for v in values if v // 2 == pair][0]


FIRST = [
    [shifted(member(vs, m), member(us, p), c) for vs in Z_SETS for us in Y_SETS]
    for c in range(C)
    for m in range(Z // 2)
    for p in range(Y // 2)
]
SECOND = [
    [shifted(v, u, c) for v in vs for u in us] for c in range(C) for vs in Z_SETS for us in Y_SETS
]


def scalar(value):
    return jnp.full((1,), value, jnp.int32)


def normalise(precond, totals, elements):
    def body(precond_ref, totals_ref, out_ref):
        total = totals_ref[pl.ds(0, 8), :]
        for i in range(1, totals_ref.shape[0] // 8):
            total = total + totals_ref[pl.ds(8 * i, 8), :]
        scale = jnp.sqrt(total[0:1, 0:1] / elements + 1e-06)
        out_ref[...] = (precond_ref[...] / scale).astype(bf16)

    return pl.pallas_call(
        body,
        in_specs=[VMEM, VMEM],
        out_specs=VMEM,
        out_shape=jax.ShapeDtypeStruct(precond.shape, bf16),
        compiler_params=pltpu.CompilerParams(vmem_limit_bytes=4 * 2**20),
        name="normalise",
    )(precond, totals)


def half_product(half, tokens, cotangent):
    depth, width = tokens.shape
    rows = width // C

    def body(half_ref, tokens_ref, cotangent_ref, out_ref, turned):
        turned[...] = tokens_ref[...].T

        for n in range(width // TILE):
            columns = pl.ds(n * TILE, TILE)
            out_ref[:, columns] = jnp.dot(
                turned[...], cotangent_ref[:, columns], preferred_element_type=f32
            )

    return pl.pallas_call(
        body,
        grid_spec=pltpu.PrefetchScalarGridSpec(
            num_scalar_prefetch=1,
            grid=(1,),
            in_specs=[
                pl.BlockSpec((depth, rows), lambda i, half: (0, half[0])),
                pl.BlockSpec((depth, width), lambda i, half: (0, 0)),
            ],
            out_specs=pl.BlockSpec((rows, width), lambda i, half: (0, 0)),
            scratch_shapes=[pltpu.VMEM((rows, depth), bf16)],
        ),
        out_shape=jax.ShapeDtypeStruct((rows, width), f32),
        compiler_params=pltpu.CompilerParams(vmem_limit_bytes=40 * 2**20),
        cost_estimate=pl.CostEstimate(
            flops=2 * depth * rows * width, bytes_accessed=6 * 2**20, transcendentals=0
        ),
        name="half_product",
    )(half, tokens, cotangent)


def dot(a, b):
    return jnp.dot(a, b, preferred_element_type=f32)


def fold(square):
    return jnp.sum(square.reshape(-1, 8, square.shape[1]), axis=0)


def own_share(mine):
    half, width = mine.shape
    lo, hi = pl.ds(0, half), pl.ds(half, half)

    def body(mine_ref, turned_ref, right_ref, left_ref):
        turned_ref[...] = mine_ref[...].T
        left_ref[...] = dot(mine_ref[...], turned_ref[...])
        right_ref[lo, lo] = dot(turned_ref[lo, :], mine_ref[:, lo])
        right_ref[:, hi] = dot(turned_ref[...], mine_ref[:, hi])

    return pl.pallas_call(
        body,
        in_specs=[VMEM],
        out_specs=[VMEM, VMEM, VMEM],
        out_shape=[
            jax.ShapeDtypeStruct((width, half), bf16),
            jax.ShapeDtypeStruct((width, width), f32),
            jax.ShapeDtypeStruct((half, half), f32),
        ],
        compiler_params=pltpu.CompilerParams(vmem_limit_bytes=24 * 2**20),
        cost_estimate=pl.CostEstimate(
            flops=2 * width**3, bytes_accessed=2**20, transcendentals=0
        ),
        name="own_share",
    )(mine)


def precondition(place, mine, theirs, turned, right, left, copies):
    half, width = mine.shape
    block = 16
    lo, hi = pl.ds(0, half), pl.ds(half, half)

    def body(place_ref, mine_ref, theirs_ref, turned_ref, right_ref, left_ref, rows_ref, square_ref, g, gt, sl, sr, xl, yl, xr, yr, f0l, f1l, f0r, f1r, h, k, theirs_turned):
        core, own = place_ref[0], place_ref[1]
        ours = pl.ds(pl.multiple_of(core * half, half), half)
        others = pl.ds(pl.multiple_of((1 - core) * half, half), half)
        g[ours, :] = mine_ref[...]
        g[others, :] = theirs_ref[...]
        row = lax.broadcasted_iota(jnp.int32, (half, half), 0)
        column = lax.broadcasted_iota(jnp.int32, (half, half), 1)
        eye = row == column

        def factor(iterate, diagonal):
            if not diagonal:
                return (iterate * -0.25).astype(bf16)
            return (jnp.where(eye, 5.0 - iterate, -iterate) * 0.25).astype(bf16)

        def inverse_norm(diagonal, above):
            acc = 2.0 * fold(above * above)
            for s in diagonal:
                acc = acc + fold(s * s)
            total = jnp.sum(jnp.sum(acc, axis=0, keepdims=True), axis=1, keepdims=True)
            return 1.0 / jnp.sqrt(total)

        def left_stat():
            s = dot(theirs_ref[...], theirs_turned[...])
            sl[others, others] = s
            sl[ours, ours] = left_ref[...]
            above = dot(g[lo, :], gt[:, hi])
            sl[lo, hi] = above
            return inverse_norm([s, left_ref[...]], above)

        def right_stat():
            first_block = right_ref[lo, lo] + dot(theirs_turned[lo, :], theirs_ref[:, lo])
            sr[lo, lo] = first_block
            s = right_ref[:, hi] + dot(theirs_turned[...], theirs_ref[:, hi])
            sr[:, hi] = s
            return inverse_norm([first_block, s[half:]], s[:half])

        def first(s, inverse, x, f):
            for r, c in ((lo, lo), (lo, hi), (hi, hi)):
                it = (s[r, c] * inverse).astype(bf16)
                x[r, c] = it
                fac = factor(it.astype(f32), r is c)
                f[r, c] = fac
                if r is not c:
                    x[c, r] = it.T
                    f[c, r] = fac.T

        def power(x, f, out):
            for c in (lo, hi):
                out[:, c] = dot(x[...], f[:, c]).astype(bf16)

        def last(x, f, out, columns):
            for c in columns:
                it = dot(x[...], f[:, c]).astype(bf16).astype(f32)
                out[lo, c] = factor(it[:half], c is lo)
                out[hi, c] = factor(it[half:], c is hi)

        theirs_turned[...] = theirs_ref[...].T
        gt[:, ours] = turned_ref[...]
        gt[:, others] = theirs_turned[...]
        inverse_l = left_stat()
        first(sl, inverse_l, xl, f0l)
        inverse_r = right_stat()
        power(xl, f0l, yl)
        first(sr, inverse_r, xr, f0r)
        power(yl, f0l, xl)
        power(xr, f0r, yr)
        power(xl, f0l, yl)
        for i in range(half // block):
            source = pl.ds(pl.multiple_of((2 * i + core) * block, block), block)
            h[pl.ds(i * block, block), :] = f0l[source, :]
        power(yr, f0r, xr)
        last(yl, f0l, f1l, (lo, hi))
        power(xr, f0r, yr)
        power(h, f1l, k)
        last(yr, f0r, f1r, (lo,))
        power(k, g, h)
        last(yr, f0r, f1r, (hi,))
        power(h, f0r, k)
        precond = sl
        acc = jnp.zeros((8, half), f32)
        for c in (lo, hi):
            p = dot(k[...], f1r[:, c])
            precond[lo, c] = p
            acc = acc + fold(p * p)
        total = jnp.sum(jnp.sum(acc, axis=0, keepdims=True), axis=1, keepdims=True)
        square_ref[...] = jnp.broadcast_to(total, square_ref.shape)
        rows_ref[...] = precond[pl.ds(pl.multiple_of(own * block, block), block), :]

    wide, stat_t = pltpu.VMEM((width, width), bf16), pltpu.VMEM((width, width), f32)
    narrow = pltpu.VMEM((half, width), bf16)
    return pl.pallas_call(
        body,
        in_specs=[SMEM] + [VMEM] * 5,
        out_specs=[VMEM, VMEM],
        out_shape=[
            jax.ShapeDtypeStruct((block, width), f32),
            jax.ShapeDtypeStruct((8 * copies, 128), f32),
        ],
        scratch_shapes=[wide, wide, stat_t, stat_t] + [wide] * 8 + [narrow] * 2 + [pltpu.VMEM((width, half), bf16)],
        compiler_params=pltpu.CompilerParams(vmem_limit_bytes=44 * 2**20),
        cost_estimate=pl.CostEstimate(
            flops=23 * width**3, bytes_accessed=3 * 2**20, transcendentals=0
        ),
        name="precondition",
    )(place, mine, theirs, turned, right, left)


def on_device(tokens, cotangent):
    width = tokens.shape[1]
    half = width // C
    z, y, c = lax.axis_index("z"), lax.axis_index("y"), lax.axis_index("c")
    core_swap = [(0, 1), (1, 0)]

    away = half_product(scalar(1 - c), tokens, cotangent)
    received = lax.ppermute(away, "c", core_swap)
    rows = half_product(scalar(c), tokens, cotangent) + received
    for groups in (FIRST, SECOND):
        count = len(groups[0])
        parts = rows.reshape(count, rows.shape[0] // count, width)
        rows = jnp.sum(lax.all_to_all(parts, DP, 0, 0, axis_index_groups=groups), axis=0)
    rows = rows.astype(bf16)
    rows = lax.all_gather(rows, DP, axis_index_groups=SECOND, axis=0, tiled=True)
    copies = jnp.broadcast_to(rows, (len(FIRST[0]),) + rows.shape)
    rows = lax.all_to_all(copies, DP, 0, 0, axis_index_groups=FIRST).reshape(half, width)
    theirs = lax.ppermute(rows, "c", core_swap)

    groups = lax.axis_size("group")
    place = jnp.stack([c, z * Y + y]).astype(jnp.int32)
    precond, square = precondition(place, rows, theirs, *own_share(rows), C * groups)
    square = square.reshape(C * groups, 8, 128)
    totals = lax.all_to_all(square, ("c", "group"), 0, 0).reshape(C * groups * 8, 128)
    return normalise(precond, totals, groups * width * width)


def solution(mesh):
    groups = mesh.shape["group"]
    split = Mesh(np.asarray(mesh.devices).reshape(Z, Y, C, groups), DP + ("group",))
    return jax.shard_map(
        on_device,
        mesh=split,
        in_specs=(P(DP, None), P(DP, "group")),
        out_specs=P(DP, "group"),
        check_vma=False,
    )
```

```python
import jax
import jax.numpy as jnp
import numpy as np
from jax import lax
from jax.experimental import pallas as pl
from jax.experimental.pallas import tpu as pltpu
from jax.sharding import Mesh, PartitionSpec as P

Z, Y, C = 4, 8, 2
DP = ("z", "y", "c")
TILE = 512
VMEM = pl.BlockSpec(memory_space=pltpu.VMEM)
SMEM = pl.BlockSpec(memory_space=pltpu.SMEM)
f32, bf16 = jnp.float32, jnp.bfloat16


def device(z, y, c):
    return z * Y * C + y * C + c


Y_SETS = ((0, 2, 5, 7), (1, 3, 4, 6))
Z_SETS = ((0, 3), (1, 2))


def shifted(v, u, c):
    return device((v + c) % Z, (u + c) % Y, c)


def member(values, pair):
    return [v for v in values if v // 2 == pair][0]


FIRST = [
    [shifted(member(vs, m), member(us, p), c) for vs in Z_SETS for us in Y_SETS]
    for c in range(C)
    for m in range(Z // 2)
    for p in range(Y // 2)
]
SECOND = [
    [shifted(v, u, c) for v in vs for u in us] for c in range(C) for vs in Z_SETS for us in Y_SETS
]


def scalar(value):
    return jnp.full((1,), value, jnp.int32)


def normalise(precond, totals, elements):
    def body(precond_ref, totals_ref, out_ref):
        total = totals_ref[pl.ds(0, 8), :]
        for i in range(1, totals_ref.shape[0] // 8):
            total = total + totals_ref[pl.ds(8 * i, 8), :]
        scale = jnp.sqrt(total[0:1, 0:1] / elements + 1e-06)
        out_ref[...] = (precond_ref[...] / scale).astype(bf16)

    return pl.pallas_call(
        body,
        in_specs=[VMEM, VMEM],
        out_specs=VMEM,
        out_shape=jax.ShapeDtypeStruct(precond.shape, bf16),
        compiler_params=pltpu.CompilerParams(vmem_limit_bytes=4 * 2**20),
        name="normalise",
    )(precond, totals)


def half_product(half, tokens, cotangent):
    depth, width = tokens.shape
    rows = width // C

    def body(half_ref, tokens_ref, cotangent_ref, out_ref, turned):
        turned[...] = tokens_ref[...].T

        for n in range(width // TILE):
            columns = pl.ds(n * TILE, TILE)
            out_ref[:, columns] = jnp.dot(
                turned[...], cotangent_ref[:, columns], preferred_element_type=f32
            )

    return pl.pallas_call(
        body,
        grid_spec=pltpu.PrefetchScalarGridSpec(
            num_scalar_prefetch=1,
            grid=(1,),
            in_specs=[
                pl.BlockSpec((depth, rows), lambda i, half: (0, half[0])),
                pl.BlockSpec((depth, width), lambda i, half: (0, 0)),
            ],
            out_specs=pl.BlockSpec((rows, width), lambda i, half: (0, 0)),
            scratch_shapes=[pltpu.VMEM((rows, depth), bf16)],
        ),
        out_shape=jax.ShapeDtypeStruct((rows, width), f32),
        compiler_params=pltpu.CompilerParams(vmem_limit_bytes=40 * 2**20),
        cost_estimate=pl.CostEstimate(
            flops=2 * depth * rows * width, bytes_accessed=6 * 2**20, transcendentals=0
        ),
        name="half_product",
    )(half, tokens, cotangent)


def product(tokens, cotangent):
    depth, rows = tokens.shape
    width = cotangent.shape[1]

    def body(tokens_ref, cotangent_ref, out_ref, turned):
        turned[...] = tokens_ref[...].T
        for n in range(width // TILE):
            columns = pl.ds(n * TILE, TILE)
            out_ref[:, columns] = jnp.dot(
                turned[...], cotangent_ref[:, columns], preferred_element_type=f32
            )

    return pl.pallas_call(
        body,
        in_specs=[VMEM] * 2,
        out_specs=VMEM,
        out_shape=jax.ShapeDtypeStruct((rows, width), f32),
        scratch_shapes=[pltpu.VMEM((rows, depth), bf16)],
        compiler_params=pltpu.CompilerParams(vmem_limit_bytes=40 * 2**20),
        cost_estimate=pl.CostEstimate(
            flops=2 * depth * rows * width, bytes_accessed=6 * 2**20, transcendentals=0
        ),
        name="product",
    )(tokens, cotangent)


def dot(a, b):
    return jnp.dot(a, b, preferred_element_type=f32)


def fold(square):
    return jnp.sum(square.reshape(-1, 8, square.shape[1]), axis=0)


def own_share(mine):
    half, width = mine.shape
    lo, hi = pl.ds(0, half), pl.ds(half, half)

    def body(mine_ref, turned_ref, right_ref, left_ref):
        turned_ref[...] = mine_ref[...].T
        left_ref[...] = dot(mine_ref[...], turned_ref[...])
        right_ref[lo, lo] = dot(turned_ref[lo, :], mine_ref[:, lo])
        right_ref[:, hi] = dot(turned_ref[...], mine_ref[:, hi])

    return pl.pallas_call(
        body,
        in_specs=[VMEM],
        out_specs=[VMEM, VMEM, VMEM],
        out_shape=[
            jax.ShapeDtypeStruct((width, half), bf16),
            jax.ShapeDtypeStruct((width, width), f32),
            jax.ShapeDtypeStruct((half, half), f32),
        ],
        compiler_params=pltpu.CompilerParams(vmem_limit_bytes=24 * 2**20),
        cost_estimate=pl.CostEstimate(
            flops=2 * width**3, bytes_accessed=2**20, transcendentals=0
        ),
        name="own_share",
    )(mine)


def precondition(place, mine, theirs, turned, right, left, copies):
    half, width = mine.shape
    block = 16
    lo, hi = pl.ds(0, half), pl.ds(half, half)

    def body(place_ref, mine_ref, theirs_ref, turned_ref, right_ref, left_ref, rows_ref, square_ref, g, gt, sl, sr, xl, yl, xr, yr, f0l, f1l, f0r, f1r, h, k, theirs_turned):
        core, own = place_ref[0], place_ref[1]
        ours = pl.ds(pl.multiple_of(core * half, half), half)
        others = pl.ds(pl.multiple_of((1 - core) * half, half), half)
        g[ours, :] = mine_ref[...]
        g[others, :] = theirs_ref[...]
        row = lax.broadcasted_iota(jnp.int32, (half, half), 0)
        column = lax.broadcasted_iota(jnp.int32, (half, half), 1)
        eye = row == column

        def factor(iterate, diagonal):
            if not diagonal:
                return (iterate * -0.25).astype(bf16)
            return (jnp.where(eye, 5.0 - iterate, -iterate) * 0.25).astype(bf16)

        def norm(diagonal, above):
            acc = 2.0 * fold(above * above)
            for s in diagonal:
                acc = acc + fold(s * s)
            total = jnp.sum(jnp.sum(acc, axis=0, keepdims=True), axis=1, keepdims=True)
            return jnp.sqrt(total)

        def left_stat():
            s = dot(theirs_ref[...], theirs_turned[...])
            sl[others, others] = s
            sl[ours, ours] = left_ref[...]
            above = dot(g[lo, :], gt[:, hi])
            sl[lo, hi] = above
            return norm([s, left_ref[...]], above)

        def right_stat():
            first_block = right_ref[lo, lo] + dot(theirs_turned[lo, :], theirs_ref[:, lo])
            sr[lo, lo] = first_block
            s = right_ref[:, hi] + dot(theirs_turned[...], theirs_ref[:, hi])
            sr[:, hi] = s
            return norm([first_block, s[half:]], s[:half])

        def first(s, size, x, f):
            for r, c in ((lo, lo), (lo, hi), (hi, hi)):
                it = (s[r, c] / size).astype(bf16)
                x[r, c] = it
                fac = factor(it.astype(f32), r is c)
                f[r, c] = fac
                if r is not c:
                    x[c, r] = it.T
                    f[c, r] = fac.T

        def power(x, f, out):
            for c in (lo, hi):
                out[:, c] = dot(x[...], f[:, c]).astype(bf16)

        def last(x, f, out):
            for c in (lo, hi):
                it = dot(x[...], f[:, c]).astype(bf16).astype(f32)
                out[lo, c] = factor(it[:half], c is lo)
                out[hi, c] = factor(it[half:], c is hi)

        theirs_turned[...] = theirs_ref[...].T
        gt[:, ours] = turned_ref[...]
        gt[:, others] = theirs_turned[...]
        norm_l = left_stat()
        first(sl, norm_l, xl, f0l)
        norm_r = right_stat()
        power(xl, f0l, yl)
        first(sr, norm_r, xr, f0r)
        power(yl, f0l, xl)
        power(xr, f0r, yr)
        power(xl, f0l, yl)
        power(yr, f0r, xr)
        last(yl, f0l, f1l)
        power(xr, f0r, yr)

        for i in range(half // block):
            source = pl.ds(pl.multiple_of((2 * i + core) * block, block), block)
            h[pl.ds(i * block, block), :] = f0l[source, :]
        power(h, f1l, k)
        last(yr, f0r, f1r)
        power(k, g, h)
        power(h, f0r, k)
        precond = sl
        acc = jnp.zeros((8, half), f32)
        for c in (lo, hi):
            p = dot(k[...], f1r[:, c])
            precond[lo, c] = p
            acc = acc + fold(p * p)
        total = jnp.sum(jnp.sum(acc, axis=0, keepdims=True), axis=1, keepdims=True)
        square_ref[...] = jnp.broadcast_to(total, square_ref.shape)
        rows_ref[...] = precond[pl.ds(pl.multiple_of(own * block, block), block), :]

    wide, stat_t = pltpu.VMEM((width, width), bf16), pltpu.VMEM((width, width), f32)
    narrow = pltpu.VMEM((half, width), bf16)
    return pl.pallas_call(
        body,
        in_specs=[SMEM] + [VMEM] * 5,
        out_specs=[VMEM, VMEM],
        out_shape=[
            jax.ShapeDtypeStruct((block, width), f32),
            jax.ShapeDtypeStruct((8 * copies, 128), f32),
        ],
        scratch_shapes=[wide, wide, stat_t, stat_t] + [wide] * 8 + [narrow] * 2 + [pltpu.VMEM((width, half), bf16)],
        compiler_params=pltpu.CompilerParams(vmem_limit_bytes=44 * 2**20),
        cost_estimate=pl.CostEstimate(
            flops=23 * width**3, bytes_accessed=3 * 2**20, transcendentals=0
        ),
        name="precondition",
    )(place, mine, theirs, turned, right, left)


def on_device(tokens, cotangent):
    width = tokens.shape[1]
    half = width // C
    z, y, c = lax.axis_index("z"), lax.axis_index("y"), lax.axis_index("c")
    core_swap = [(0, 1), (1, 0)]

    their_cotangent = lax.ppermute(cotangent, "c", core_swap)
    away = lax.dynamic_slice_in_dim(tokens, (1 - c) * half, half, 1)
    their_tokens = lax.ppermute(away, "c", core_swap)
    rows = half_product(scalar(c), tokens, cotangent) + product(their_tokens, their_cotangent)
    for groups in (FIRST, SECOND):
        count = len(groups[0])
        parts = rows.reshape(count, rows.shape[0] // count, width)
        rows = jnp.sum(lax.all_to_all(parts, DP, 0, 0, axis_index_groups=groups), axis=0)
    rows = rows.astype(bf16)
    for groups in (SECOND, FIRST):
        count = len(groups[0])
        copies = jnp.broadcast_to(rows, (count,) + rows.shape)
        rows = lax.all_to_all(copies, DP, 0, 0, axis_index_groups=groups)
        rows = rows.reshape(count * rows.shape[1], width)
    theirs = lax.ppermute(rows, "c", core_swap)

    groups = lax.axis_size("group")
    place = jnp.stack([c, z * Y + y]).astype(jnp.int32)
    precond, square = precondition(place, rows, theirs, *own_share(rows), C * groups)
    square = square.reshape(C * groups, 8, 128)
    totals = lax.all_to_all(square, ("c", "group"), 0, 0).reshape(C * groups * 8, 128)
    return normalise(precond, totals, groups * width * width)


def solution(mesh):
    groups = mesh.shape["group"]
    split = Mesh(np.asarray(mesh.devices).reshape(Z, Y, C, groups), DP + ("group",))
    return jax.shard_map(
        on_device,
        mesh=split,
        in_specs=(P(DP, None), P(DP, "group")),
        out_specs=P(DP, "group"),
        check_vma=False,
    )
```
